32 devices in a mesh: dp: 8 (over y, x, core), tensor: 4 (over z).
Axes of the slice: x: 2, y: 2, z: 4, core: 2. Of those that a mesh axis runs over, the one named last changes fastest.
Arguments:
- x_in: bfloat16 [8192, 8192], P(('dp', 'tensor')), may hold values from -6 to 6
- z_in: bfloat16 [8192, 8192], P(('dp', 'tensor')), may hold values from -6 to 6
- bc_in: bfloat16 [8192, 2048], P(('dp', 'tensor')), may hold values from -6 to 6
- dt_in: bfloat16 [8192, 128], P(('dp', 'tensor')), may hold values from -4 to 4
- conv_x_param: float32 [5, 8192], P(None, 'tensor'), may hold values from -3 to 3
- conv_bc_param: float32 [5, 2048], P(None, 'tensor'), may hold values from -3 to 3
- decay_rate: float32 [128], P('tensor'), may hold values from 0.01 to 2
- dt_bias: float32 [128], P('tensor'), may hold values from -3 to 0
- skip_gain: float32 [128], P('tensor'), may hold values from -3 to 3
- norm_gain: float32 [8192], P('tensor'), may hold values from 0.5 to 1.5
- ssm_state: float32 [32, 128, 64, 128], P('dp', 'tensor'), may hold values from -0.6 to 0.6
- conv_x_state: float32 [32, 3, 8192], P('dp', None, 'tensor'), may hold values from -6 to 6
- conv_bc_state: float32 [32, 3, 2048], P('dp', None, 'tensor'), may hold values from -6 to 6
- lengths: int32 [32], replicated, may hold values from 3 to 640, as said below
- prefill_owner: int32 [32], replicated, may hold values from 0 to 7, as said below
- row_start: int32 [32], replicated, may hold values from 0 to 1021, as said below
Outputs:
- y_out: bfloat16 [8192, 8192], P('dp', 'tensor')
- new_ssm_state: float32 [32, 128, 64, 128], P('dp', 'tensor')
- new_conv_x_state: float32 [32, 3, 8192], P('dp', None, 'tensor')
- new_conv_bc_state: float32 [32, 3, 2048], P('dp', None, 'tensor')
The draws below stay inside these ranges and needn't reach their ends.
Inputs may be any that keep to these rules, and one draw needn't show every extreme that they name: `prefill_owner`: conversation c is held by index c // 4 along dp. Of the 4 conversations of one index, two are prefilled there, one on the next index and one on the previous index, cyclically; so every index prefills 4 conversations. The lengths of the conversations of one prefill owner add up to 1024. `row_start`: the conversations of one prefill owner cover its 1024 rows in consecutive runs, each row in exactly one.
All inputs are finite; a program needn't handle non-finite values.
Results may differ from the reference program's by a relative error of at most 0.005.
Values may be sent and summed in bfloat16 or wider, within the bound.
A program may use at most 128 MiB of HBM per device.

```python
import math
import jax
import jax.numpy as jnp
from jax import lax

HEADS = 128
HEADDIM = 64
STATE = 128
GROUPS = 8
SLOTS = 4
ROWS = 1024
MAXLEN = 640
HD = 8192
BCW = 2048
CONVS = 32
TOKENS = 8192
N_DP = 8


def plan_tables(key):
    rank_scores = jax.random.randint(jax.random.fold_in(key, 11), (N_DP, SLOTS), 0, 1 << 20) * SLOTS + jnp.arange(SLOTS, dtype=jnp.int32)[None, :]
    order_idx = jnp.argsort(rank_scores, axis=1)
    role_table = jnp.array([0, 0, 1, 2], dtype=jnp.int32)
    roles = role_table[order_idx]
    weights = jax.random.randint(jax.random.fold_in(key, 12), (N_DP, SLOTS), 16, 64)
    shares = weights * (ROWS - SLOTS) // jnp.sum(weights, axis=1, keepdims=True) + 1
    leading = ROWS - jnp.sum(shares[:, 1:], axis=1)
    shares = jnp.concatenate([leading[:, None], shares[:, 1:]], axis=1)
    longest_owner = jax.random.randint(jax.random.fold_in(key, 13), (), 0, N_DP)
    rest_piece = (ROWS - MAXLEN - 3) // 2
    special = jnp.array([MAXLEN, rest_piece, ROWS - MAXLEN - 3 - rest_piece, 3], dtype=jnp.int32)
    owner_rows = jnp.arange(N_DP, dtype=jnp.int32)[:, None]
    shares = jnp.where(owner_rows == longest_owner, special[None, :], shares)
    firsts = jnp.cumsum(shares, axis=1) - shares
    stay_rank = jnp.cumsum((roles == 0).astype(jnp.int32), axis=1) - 1
    owner_idx = jnp.where(roles == 0, owner_rows, jnp.where(roles == 1, (owner_rows + 1) % N_DP, (owner_rows + N_DP - 1) % N_DP))
    slot_idx = jnp.where(roles == 0, stay_rank, jnp.where(roles == 1, 2, 3))
    return (shares[owner_idx, slot_idx].reshape(-1), owner_idx.reshape(-1), firsts[owner_idx, slot_idx].reshape(-1))


def draw_lengths(key, part):
    tables = plan_tables(key)
    return tables[0].astype(jnp.int32)


def draw_prefill_owner(key, part):
    tables = plan_tables(key)
    return tables[1].astype(jnp.int32)


def draw_row_start(key, part):
    tables = plan_tables(key)
    return tables[2].astype(jnp.int32)


def steps_of(rng, shape, split, smallest, high):
    level = 1.0
    for dim, blocks in split:
        heights = jax.random.uniform(jax.random.fold_in(jax.random.fold_in(rng, 6), dim), (blocks,), jnp.float32, smallest / len(split), high / len(split))
        level = level * jnp.repeat(jnp.exp(heights), shape[dim] // blocks).reshape((-1,) + (1,) * (len(shape) - 1 - dim))
    return level


def bell_draw(rng, extent, deviation, bound, split=(), kind=jnp.bfloat16):
    factor_of = steps_of(rng, extent, split, -0.22, 0.18) if split else 1.0
    drawn = jax.random.normal(rng, extent, jnp.float32) * deviation * factor_of
    return jnp.minimum(jnp.maximum(drawn, -bound), bound).astype(kind)


def setup_inputs(seed: int = 0) -> dict:
    key_of = jax.random.split(jax.random.key(seed), 17)
    return {
        "x_in": bell_draw(key_of[0], (TOKENS, HD), 1.0, 6.0, ((0, 32),)),
        "z_in": bell_draw(key_of[1], (TOKENS, HD), 1.0, 6.0, ((0, 32),)),
        "bc_in": bell_draw(key_of[2], (TOKENS, BCW), 1.0, 6.0, ((0, 32),)),
        "dt_in": bell_draw(key_of[3], (TOKENS, HEADS), 1.0, 4.0, ((0, 32),)),
        "conv_x_param": bell_draw(key_of[4], (5, HD), 0.5, 3.0, ((1, 4),), jnp.float32),
        "conv_bc_param": bell_draw(key_of[5], (5, BCW), 0.5, 3.0, ((1, 4),), jnp.float32),
        "decay_rate": jnp.clip(jnp.exp(math.log(2.0) - 5.2983174 * jax.random.uniform(key_of[6], (HEADS,), jnp.float32) ** steps_of(key_of[6], (HEADS,), ((0, 4),), -0.2, 0.2)), 0.01, 2.0),
        "dt_bias": jnp.clip(-3.0 + 3.0 * jax.random.uniform(key_of[7], (HEADS,), jnp.float32) ** steps_of(key_of[7], (HEADS,), ((0, 4),), -0.2, 0.2), -3.0, 0.0),
        "skip_gain": bell_draw(key_of[8], (HEADS,), 1.0, 3.0, ((0, 4),), jnp.float32),
        "norm_gain": jnp.clip(1.0 + 0.1 * jax.random.normal(key_of[9], (HD,), jnp.float32), 0.5, 1.5),
        "ssm_state": bell_draw(key_of[10], (CONVS, HEADS, HEADDIM, STATE), 0.1, 0.6, ((0, 8), (1, 4)), jnp.float32),
        "conv_x_state": bell_draw(key_of[11], (CONVS, 3, HD), 1.0, 6.0, ((0, 8), (2, 4)), jnp.float32),
        "conv_bc_state": bell_draw(key_of[12], (CONVS, 3, BCW), 1.0, 6.0, ((0, 8), (2, 4)), jnp.float32),
        "lengths": draw_lengths(jax.random.fold_in(key_of[16], 71), 0),
        "prefill_owner": draw_prefill_owner(jax.random.fold_in(key_of[16], 71), 0),
        "row_start": draw_row_start(jax.random.fold_in(key_of[16], 71), 0),
    }


EPSILON = 1e-05
best_precision = lax.Precision.HIGHEST

def plan_rows(owner_idx, lengths, prefill_owner, row_start, row_count):
    conv_ids = jnp.nonzero(prefill_owner == owner_idx, size=SLOTS)[0].astype(jnp.int32)
    order_idx = jnp.argsort(row_start[conv_ids]).astype(jnp.int32)
    conv_ids = conv_ids[order_idx]
    starts = row_start[conv_ids]
    seg_lengths = lengths[conv_ids]
    row_idx = jnp.arange(row_count, dtype=jnp.int32)
    inside = (row_idx[:, None] >= starts[None, :]) & (row_idx[:, None] < (starts + seg_lengths)[None, :])
    segment = lax.optimization_barrier(jnp.sum(jnp.where(inside, jnp.arange(SLOTS, dtype=jnp.int32)[None, :], 0), axis=1))
    position = row_idx - lax.optimization_barrier(jnp.sum(jnp.where(inside, starts[None, :], 0), axis=1))
    same_tri = (segment[:, None] == segment[None, :]) & (row_idx[None, :] <= row_idx[:, None])
    return (conv_ids, starts, seg_lengths, inside, position, same_tri)

def causal_conv(values, param, state, inside, position):
    row_count, channels = values.shape
    result = param[4][None, :] + param[3][None, :] * values
    for lag_rows in (1, 2, 3):
        shifted = jnp.concatenate([jnp.zeros((lag_rows, channels), jnp.float32), values[:-lag_rows]], axis=0)
        picker = inside[:, :, None] & ((3 - lag_rows + position)[:, None, None] == jnp.arange(3, dtype=jnp.int32)[None, None, :])
        from_state = jnp.dot(picker.astype(jnp.float32).reshape(row_count, SLOTS * 3), state.reshape(SLOTS * 3, channels), precision=best_precision, preferred_element_type=jnp.float32)
        previous = jnp.where((position >= lag_rows)[:, None], shifted, from_state)
        result = result + param[3 - lag_rows][None, :] * previous
    return result

def last_inputs(values, starts, seg_lengths):
    row_idx = jnp.arange(values.shape[0], dtype=jnp.int32)
    target = (starts + seg_lengths)[:, None] - 3 + jnp.arange(3, dtype=jnp.int32)[None, :]
    picker = (target[:, :, None] == row_idx[None, None, :]).astype(jnp.float32).reshape(SLOTS * 3, values.shape[0])
    taken = jnp.dot(picker, values, precision=best_precision, preferred_element_type=jnp.float32)
    return taken.reshape(SLOTS, 3, values.shape[1])

def head_scan(x_head, dt_head, decay_speed, skip_value, mix_matrix, c_half, b_half, initial_head, inside, starts, seg_lengths, same_tri):
    log_decay = -dt_head * decay_speed
    running = jnp.cumsum(log_decay)
    before = running[starts] - log_decay[starts]
    cumulated = running - lax.optimization_barrier(jnp.sum(jnp.where(inside, before[None, :], 0.0), axis=1))
    end_decay = running[starts + seg_lengths - 1] - before
    spread = jnp.where(same_tri, cumulated[:, None] - cumulated[None, :], 0.0)
    decay_matrix = jnp.where(same_tri, jnp.exp(spread), 0.0)
    scores = (mix_matrix * decay_matrix * dt_head[None, :]).astype(jnp.bfloat16)
    output = jnp.dot(scores, x_head, preferred_element_type=jnp.float32)
    state_rows = jnp.transpose(initial_head, (2, 0, 1)).reshape(initial_head.shape[2], SLOTS * HEADDIM)
    state_hi = state_rows.astype(jnp.bfloat16)
    state_lo = (state_rows - lax.optimization_barrier(state_hi).astype(jnp.float32)).astype(jnp.bfloat16)
    initial_term = jnp.dot(c_half, state_hi, preferred_element_type=jnp.float32) + jnp.dot(c_half, state_lo, preferred_element_type=jnp.float32)
    initial_term = lax.optimization_barrier(jnp.sum(jnp.where(inside[:, :, None], initial_term.reshape(-1, SLOTS, HEADDIM), 0.0), axis=1))
    x_wide = x_head.astype(jnp.float32)
    output = output + jnp.exp(cumulated)[:, None] * initial_term + skip_value * x_wide
    row_end = lax.optimization_barrier(jnp.sum(jnp.where(inside, end_decay[None, :], 0.0), axis=1))
    carried = (x_wide * (jnp.exp(row_end - cumulated) * dt_head)[:, None]).astype(jnp.bfloat16)
    b_slots = jnp.where(inside[:, :, None], b_half[:, None, :], jnp.zeros((), jnp.bfloat16)).reshape(b_half.shape[0], -1)
    final_state = jnp.dot(carried.T, b_slots, preferred_element_type=jnp.float32).reshape(HEADDIM, SLOTS, -1)
    final_state = jnp.transpose(final_state, (1, 0, 2)) + jnp.exp(end_decay)[:, None, None] * initial_head
    return (output, final_state)

def group_block(x_group, z_group, bc_group, dt_group, rate_group, skip_group, gain_group, initial_group, inside, starts, seg_lengths, same_tri):
    b_half = bc_group[:, :STATE]
    c_half = bc_group[:, STATE:]
    mix_matrix = jnp.dot(c_half, b_half.T, preferred_element_type=jnp.float32)

    def one_head(head_idx):
        x_head = lax.dynamic_slice_in_dim(x_group, head_idx * HEADDIM, HEADDIM, 1)
        dt_head = lax.dynamic_index_in_dim(dt_group, head_idx, 1, keepdims=False)
        decay_speed = lax.dynamic_index_in_dim(rate_group, head_idx, 0, keepdims=False)
        skip_value = lax.dynamic_index_in_dim(skip_group, head_idx, 0, keepdims=False)
        initial_head = lax.dynamic_index_in_dim(initial_group, head_idx, 1, keepdims=False)
        return head_scan(x_head, dt_head, decay_speed, skip_value, mix_matrix, c_half, b_half, initial_head, inside, starts, seg_lengths, same_tri)
    head_outputs, head_states = lax.map(one_head, jnp.arange(HEADS // GROUPS, dtype=jnp.int32))
    joined = jnp.transpose(head_outputs, (1, 0, 2)).reshape(head_outputs.shape[1], -1)
    gated = joined * jax.nn.silu(z_group.astype(jnp.float32))
    mean_square = lax.optimization_barrier(jnp.mean(gated * gated, axis=1, keepdims=True))
    normed = (gated * lax.rsqrt(mean_square + EPSILON) * gain_group[None, :]).astype(jnp.bfloat16)
    return (normed, jnp.transpose(head_states, (1, 0, 2, 3)))

def mixer(x_rows, z_rows, bc_rows, dt_rows, conv_x_param, conv_bc_param, decay_rate, dt_bias, skip_gain, norm_gain, initial_ssm, initial_cx, initial_cbc, inside, position, starts, seg_lengths, same_tri):
    x_values = x_rows.astype(jnp.float32)
    bc_values = bc_rows.astype(jnp.float32)
    x_conv = jax.nn.silu(causal_conv(x_values, conv_x_param, initial_cx, inside, position)).astype(jnp.bfloat16)
    bc_conv = jax.nn.silu(causal_conv(bc_values, conv_bc_param, initial_cbc, inside, position)).astype(jnp.bfloat16)
    dt_all = jax.nn.softplus(dt_rows.astype(jnp.float32) + dt_bias[None, :])
    per_group = HEADS // GROUPS
    group_count = dt_rows.shape[1] // per_group
    outputs = []
    finals = []
    for group_idx in range(group_count):
        col_lo = group_idx * per_group * HEADDIM
        col_hi = col_lo + per_group * HEADDIM
        head_lo = group_idx * per_group
        head_hi = head_lo + per_group
        bc_lo = group_idx * 2 * STATE
        normed, final_group = group_block(x_conv[:, col_lo:col_hi], z_rows[:, col_lo:col_hi], bc_conv[:, bc_lo:bc_lo + 2 * STATE], dt_all[:, head_lo:head_hi], decay_rate[head_lo:head_hi], skip_gain[head_lo:head_hi], norm_gain[col_lo:col_hi], initial_ssm[:, head_lo:head_hi], inside, starts, seg_lengths, same_tri)
        outputs.append(normed)
        finals.append(final_group)
    y_block = jnp.concatenate(outputs, axis=1)
    final_ssm = jnp.concatenate(finals, axis=1)
    return (y_block, final_ssm, last_inputs(x_values, starts, seg_lengths), last_inputs(bc_values, starts, seg_lengths))

def reference(x_in, z_in, bc_in, dt_in, conv_x_param, conv_bc_param, decay_rate, dt_bias, skip_gain, norm_gain, ssm_state, conv_x_state, conv_bc_state, lengths, prefill_owner, row_start):

    def one_owner(owner_idx):
        conv_ids, starts, seg_lengths, inside, position, same_tri = plan_rows(owner_idx, lengths, prefill_owner, row_start, ROWS)
        first_row = (owner_idx * ROWS).astype(jnp.int32)

        def take_rows(source):
            return lax.dynamic_slice_in_dim(source, first_row, ROWS, 0)
        y_block, final_ssm, final_cx, final_cbc = mixer(take_rows(x_in), take_rows(z_in), take_rows(bc_in), take_rows(dt_in), conv_x_param, conv_bc_param, decay_rate, dt_bias, skip_gain, norm_gain, ssm_state[conv_ids], conv_x_state[conv_ids], conv_bc_state[conv_ids], inside, position, starts, seg_lengths, same_tri)
        return (y_block, final_ssm, final_cx, final_cbc, conv_ids)
    y_all, ssm_all, cx_all, cbc_all, ids_all = lax.map(one_owner, jnp.arange(N_DP, dtype=jnp.int32))
    flat_ids = ids_all.reshape(-1)
    new_ssm = jnp.zeros_like(ssm_state).at[flat_ids].set(ssm_all.reshape((-1,) + ssm_state.shape[1:]))
    new_cx = jnp.zeros_like(conv_x_state).at[flat_ids].set(cx_all.reshape((-1,) + conv_x_state.shape[1:]))
    new_cbc = jnp.zeros_like(conv_bc_state).at[flat_ids].set(cbc_all.reshape((-1,) + conv_bc_state.shape[1:]))
    return (y_all.reshape(TOKENS, HD), new_ssm, new_cx, new_cbc)
```

```python
import functools

import jax
import jax.numpy as jnp
from jax import lax
from jax.experimental import pallas as pl
from jax.experimental.pallas import tpu as pltpu
from jax.sharding import PartitionSpec as P

HEADS = 128
HEADDIM = 64
STATE = 128
GROUPS = 8
SLOTS = 4
PER_GROUP = HEADS // GROUPS
WIDTH = PER_GROUP * HEADDIM
CHUNK = 256
LANES = 128
EPSILON = 1e-05
LOG2E = 1.4426950408889634
F32 = jnp.float32
BF16 = jnp.bfloat16
best_precision = lax.Precision.HIGHEST


def silu(value):
    half = 0.5 * value
    return half + half * jnp.tanh(half)


def parts_of(value, count):
    parts = []
    for _ in range(count):
        part = value.astype(BF16)
        parts.append(part)
        value = value - part.astype(F32)
    return jnp.concatenate(parts, axis=-1)


def dot(a, b):
    return jnp.dot(a, b, preferred_element_type=F32)


def scan_kernel(
    idx_ref,
    x_ref,
    bc_ref,
    dt_ref,
    log_ref,
    segc_ref,
    segr_ref,
    pos_ref,
    pick_ref,
    fix_x_ref,
    fix_bc_ref,
    par_x_ref,
    par_bc_ref,
    skip_ref,
    spread_ref,
    init0,
    init1,
    init2,
    init3,
    y_ref,
    fin_ref,
    state,
    xs,
    bs,
    xb,
    inter,
):
    chunk = pl.program_id(1)
    inits = (init0, init1, init2, init3)

    @pl.when(chunk == 0)
    def _():
        for k in range(SLOTS):
            state[k * STATE : (k + 1) * STATE, :] = inits[k][0].T
        xs[0:8, :] = jnp.zeros((8, xs.shape[1]), F32)
        bs[0:8, :] = jnp.zeros((8, bs.shape[1]), F32)

    @pl.when(chunk > 0)
    def _():
        xs[0:8, :] = xs[CHUNK : CHUNK + 8, :]
        bs[0:8, :] = bs[CHUNK : CHUNK + 8, :]

    xs[8 : CHUNK + 8, :] = x_ref[...].astype(F32)
    bs[8 : CHUNK + 8, :] = bc_ref[...].astype(F32)
    pos = pos_ref[...]
    pick = pick_ref[...]

    def conv(src, par_ref, fix_ref, lo):
        cols = slice(lo, lo + LANES)
        total = dot(pick, fix_ref[:, cols]) + par_ref[4:5, cols]
        total = total + par_ref[3:4, cols] * src[8 : CHUNK + 8, cols]
        for lag in (1, 2, 3):
            before = jnp.where(pos >= lag, src[8 - lag : CHUNK + 8 - lag, cols], 0.0)
            total = total + par_ref[3 - lag : 4 - lag, cols] * before
        return silu(total)

    for lo in range(0, WIDTH, LANES):
        xb[:, lo : lo + LANES] = conv(xs, par_x_ref, fix_x_ref, lo).astype(BF16)
    b_half = conv(bs, par_bc_ref, fix_bc_ref, 0).astype(BF16)
    c_half = conv(bs, par_bc_ref, fix_bc_ref, STATE).astype(BF16)
    b_wide = b_half.astype(F32)
    c_wide = c_half.astype(F32)

    segc = segc_ref[...]
    segr = segr_ref[0:1, :]
    same = jnp.concatenate([segc, segc], axis=1) == segr
    row = lax.broadcasted_iota(jnp.int32, (CHUNK, CHUNK), 0)
    col = lax.broadcasted_iota(jnp.int32, (CHUNK, CHUNK), 1)
    tri = same & (col <= row)
    upto = jnp.where(tri, 1.0, 0.0).astype(BF16)
    after = jnp.where(same & (col > row), 1.0, 0.0).astype(BF16)
    slot = lax.broadcasted_iota(jnp.int32, (8, CHUNK), 0).astype(F32)
    owned = jnp.where(slot == segr, 1.0, 0.0).astype(BF16)

    logs = parts_of(log_ref[0], 3)

    def summed(mask):
        three = dot(mask, logs)
        return three[:, :LANES] + three[:, LANES : 2 * LANES] + three[:, 2 * LANES :]

    spread = spread_ref[...]

    def expanded(value):
        return dot(parts_of(value, 2), spread)

    dt = dt_ref[0]
    grown = summed(upto)
    back = (grown - jnp.log2(dt)).T
    into = expanded(jnp.exp2(summed(after)) * dt)
    keep = expanded(jnp.exp2(summed(owned)))

    mix = lax.dot_general(c_half, b_half, (((1,), (1,)), ((), ())), preferred_element_type=F32)
    mix = jnp.where(tri, mix, 0.0)
    c_slots = jnp.concatenate(
        [jnp.where(segc == k, c_wide, 0.0).astype(BF16) for k in range(SLOTS)], axis=1
    )
    inter[...] = dot(c_slots, state[...].astype(BF16)) * expanded(jnp.exp2(grown))

    b_turned = b_wide.T
    b_slots = jnp.concatenate(
        [jnp.where(segr == k, b_turned, 0.0).astype(BF16) for k in range(SLOTS)], axis=0
    )
    carried = (xb[...].astype(F32) * into).astype(BF16)
    update = dot(b_slots, carried)
    for k in range(SLOTS):
        rows = slice(k * STATE, (k + 1) * STATE)
        state[rows, :] = state[rows, :] * keep[k : k + 1, :] + update[rows, :]

    left_lanes = lax.broadcasted_iota(jnp.int32, (CHUNK, LANES), 1) < HEADDIM
    for pair in range(PER_GROUP // 2):
        cols = slice(pair * LANES, (pair + 1) * LANES)
        xp = xb[:, cols]
        both = []
        for h in (2 * pair, 2 * pair + 1):
            gap = jnp.minimum(grown[:, h : h + 1] - back[h : h + 1, :], 64.0)
            both.append(dot((mix * jnp.exp2(gap)).astype(BF16), xp))
        y = jnp.where(left_lanes, both[0], both[1])
        y_ref[:, cols] = y + inter[:, cols] + skip_ref[0:1, cols] * xp.astype(F32)

    @pl.when(chunk == pl.num_programs(1) - 1)
    def _():
        for k in range(SLOTS):
            fin_ref[k] = state[k * STATE : (k + 1) * STATE, :].T


def gate_kernel(y_ref, z_ref, gain_ref, out_ref):
    gated = y_ref[...] * silu(z_ref[...].astype(F32))
    square = jnp.mean(gated * gated, axis=1, keepdims=True)
    out_ref[...] = (gated * lax.rsqrt(square + EPSILON) * gain_ref[...]).astype(BF16)


def run_scan(idx, x_rows, bc_rows, dt, logs, segc, segr, pos, pick, fix_x, fix_bc, par_x, par_bc, skip, states):
    rows = x_rows.shape[0]
    groups = x_rows.shape[1] // WIDTH
    chunks = rows // CHUNK
    heads = jnp.arange(2 * LANES, dtype=jnp.int32)[:, None] % LANES
    spread = (heads == jnp.arange(WIDTH, dtype=jnp.int32)[None, :] // HEADDIM).astype(BF16)

    def by_rows(width):
        return pl.BlockSpec((CHUNK, width), lambda g, c, idx: (c, 0))

    def by_both(width):
        return pl.BlockSpec((CHUNK, width), lambda g, c, idx: (c, g))

    def by_group(height, width):
        return pl.BlockSpec((height, width), lambda g, c, idx: (0, g))

    def init(k):
        return pl.BlockSpec((1, WIDTH, STATE), lambda g, c, idx: (idx[k], g, 0))

    per_group = pl.BlockSpec((1, CHUNK, LANES), lambda g, c, idx: (g, c, 0))
    grid_spec = pltpu.PrefetchScalarGridSpec(
        num_scalar_prefetch=1,
        grid=(groups, chunks),
        in_specs=[
            by_both(WIDTH),
            by_both(2 * STATE),
            per_group,
            per_group,
            by_rows(LANES),
            pl.BlockSpec((8, CHUNK), lambda g, c, idx: (0, c)),
            by_rows(LANES),
            by_rows(32),
            by_group(32, WIDTH),
            by_group(32, 2 * STATE),
            by_group(5, WIDTH),
            by_group(5, 2 * STATE),
            by_group(1, WIDTH),
            pl.BlockSpec((2 * LANES, WIDTH), lambda g, c, idx: (0, 0)),
            init(0),
            init(1),
            init(2),
            init(3),
        ],
        out_specs=[
            by_both(WIDTH),
            pl.BlockSpec((SLOTS, WIDTH, STATE), lambda g, c, idx: (0, g, 0)),
        ],
        scratch_shapes=[
            pltpu.VMEM((SLOTS * STATE, WIDTH), F32),
            pltpu.VMEM((CHUNK + 8, WIDTH), F32),
            pltpu.VMEM((CHUNK + 8, 2 * STATE), F32),
            pltpu.VMEM((CHUNK, WIDTH), BF16),
            pltpu.VMEM((CHUNK, WIDTH), F32),
        ],
    )
    return pl.pallas_call(
        scan_kernel,
        grid_spec=grid_spec,
        out_shape=[
            jax.ShapeDtypeStruct((rows, groups * WIDTH), F32),
            jax.ShapeDtypeStruct((SLOTS, groups * WIDTH, STATE), F32),
        ],
        compiler_params=pltpu.CompilerParams(
            dimension_semantics=("arbitrary", "arbitrary"), vmem_limit_bytes=48 << 20
        ),
        cost_estimate=pl.CostEstimate(
            flops=40_000_000_000, bytes_accessed=30 << 20, transcendentals=20_000_000
        ),
        name="scan",
    )(idx, x_rows, bc_rows, dt, logs, segc, segr, pos, pick, fix_x, fix_bc, par_x, par_bc, skip, spread, states, states, states, states)


def run_gate(y, z_rows, gain):
    rows, width = y.shape
    block = pl.BlockSpec((CHUNK, WIDTH), lambda g, c: (c, g))
    return pl.pallas_call(
        gate_kernel,
        grid=(width // WIDTH, rows // CHUNK),
        in_specs=[block, block, pl.BlockSpec((1, WIDTH), lambda g, c: (0, g))],
        out_specs=block,
        out_shape=jax.ShapeDtypeStruct((rows, width), BF16),
        compiler_params=pltpu.CompilerParams(
            dimension_semantics=("arbitrary", "arbitrary"), vmem_limit_bytes=32 << 20
        ),
        cost_estimate=pl.CostEstimate(
            flops=40_000_000, bytes_accessed=16 << 20, transcendentals=2_000_000
        ),
        name="gate",
    )(y, z_rows, gain[None, :])


def shifted(value, axis, steps):
    count = lax.axis_size(axis)
    pairs = [(source, (source + steps) % count) for source in range(count)]
    return lax.ppermute(value, axis, pairs)


def exchanged(value):
    return lax.all_to_all(value, "tensor", split_axis=1, concat_axis=0, tiled=True)


def plan_rows(owner_idx, lengths, prefill_owner, row_start):
    match = prefill_owner == owner_idx
    earlier = match[None, :] & (row_start[None, :] < row_start[:, None])
    rank = jnp.sum(earlier.astype(jnp.int32), axis=1)
    chosen = match[None, :] & (rank[None, :] == jnp.arange(SLOTS, dtype=jnp.int32)[:, None])

    def pick(values):
        return jnp.sum(jnp.where(chosen, values[None, :], 0), axis=1)

    ids = jnp.arange(prefill_owner.shape[0], dtype=jnp.int32)
    return pick(ids), pick(row_start), pick(lengths)


def fixes(param, state):
    rows = []
    for at in range(3):
        rows.append(sum(param[3 - lag][None, :] * state[:, 3 - lag + at] for lag in range(at + 1, 4)))
    fix = jnp.stack(rows, axis=1).reshape(SLOTS * 3, -1)
    fix = jnp.pad(fix, ((0, 4), (0, 0)))
    high = fix.astype(BF16)
    low = (fix - lax.optimization_barrier(high).astype(F32)).astype(BF16)
    return jnp.concatenate([high, low], axis=0)


def shards(
    x_in,
    z_in,
    bc_in,
    dt_in,
    conv_x_param,
    conv_bc_param,
    decay_rate,
    dt_bias,
    skip_gain,
    norm_gain,
    ssm_state,
    conv_x_state,
    conv_bc_state,
    lengths,
    prefill_owner,
    row_start,
):
    dp_count = lax.axis_size("dp")
    my_index = lax.axis_index("dp")
    left_index = (my_index + dp_count - 1) % dp_count
    right_index = (my_index + 1) % dp_count
    slot_iota = jnp.arange(SLOTS, dtype=jnp.int32)
    my_dest = lax.dynamic_slice_in_dim(prefill_owner, my_index * SLOTS, SLOTS)
    right_slot = jnp.sum(jnp.where(my_dest == right_index, slot_iota, 0))
    left_slot = jnp.sum(jnp.where(my_dest == left_index, slot_iota, 0))
    conv_ids, starts, seg_lengths = plan_rows(my_index, lengths, prefill_owner, row_start)
    homes = conv_ids // SLOTS

    heads = ssm_state.shape[1]
    channels = heads * HEADDIM
    groups = heads // PER_GROUP
    own = ssm_state.reshape(SLOTS, channels, STATE)
    own_conv = jnp.concatenate([conv_x_state, conv_bc_state], axis=2)

    def taken(array, index):
        return lax.dynamic_slice_in_dim(array, index, 1, 0)

    from_left = shifted(taken(own, right_slot), "dp", 1)
    from_right = shifted(taken(own, left_slot), "dp", -1)
    conv_left = shifted(taken(own_conv, right_slot), "dp", 1)
    conv_right = shifted(taken(own_conv, left_slot), "dp", -1)

    dt_rows = exchanged(dt_in)
    bc_rows = exchanged(bc_in)
    x_rows = exchanged(x_in)
    z_tied, x_rows, bc_rows, dt_rows = lax.optimization_barrier((z_in, x_rows, bc_rows, dt_rows))
    z_rows = exchanged(z_tied)
    row_count = x_rows.shape[0]

    states = jnp.concatenate([own, from_left, from_right], axis=0)
    where_from = jnp.where(
        homes == my_index, conv_ids % SLOTS, jnp.where(homes == left_index, SLOTS, SLOTS + 1)
    ).astype(jnp.int32)
    convs = jnp.concatenate([own_conv, conv_left, conv_right], axis=0)
    initial_conv = jnp.concatenate([taken(convs, where_from[k]) for k in range(SLOTS)], axis=0)

    row_idx = jnp.arange(row_count, dtype=jnp.int32)
    segment = jnp.sum((row_idx[:, None] >= starts[None, :]).astype(jnp.int32), axis=1) - 1
    begin = jnp.max(jnp.where(row_idx[:, None] >= starts[None, :], starts[None, :], 0), axis=1)
    position = row_idx - begin
    segc = jnp.broadcast_to(segment.astype(F32)[:, None], (row_count, LANES))
    segr = jnp.broadcast_to(segment.astype(F32)[None, :], (8, row_count))
    pos = jnp.broadcast_to(position[:, None], (row_count, LANES))
    code = jnp.where(position < 3, segment * 3 + position, 15)
    pick = (code[:, None] == jnp.arange(32, dtype=jnp.int32)[None, :] % 16).astype(BF16)

    def grouped(value, fill):
        value = jnp.transpose(value.reshape(row_count, groups, PER_GROUP), (1, 0, 2))
        return jnp.pad(value, ((0, 0), (0, 0), (0, LANES - PER_GROUP)), constant_values=fill)

    dt = jax.nn.softplus(dt_rows.astype(F32) + dt_bias[None, :])
    logs = dt * (decay_rate * (-LOG2E))[None, :]
    y, finals = run_scan(
        where_from,
        x_rows,
        bc_rows,
        grouped(dt, 1.0),
        grouped(logs, 0.0),
        segc,
        segr,
        pos,
        pick,
        fixes(conv_x_param, initial_conv[:, :, :channels]),
        fixes(conv_bc_param, initial_conv[:, :, channels:]),
        conv_x_param,
        conv_bc_param,
        jnp.repeat(skip_gain, HEADDIM)[None, :],
        states,
    )
    y_out = run_gate(y, z_rows, norm_gain)

    lasts = []
    for k in range(SLOTS):
        at = starts[k] + seg_lengths[k] - 3
        lasts.append(
            jnp.concatenate(
                [
                    lax.dynamic_slice_in_dim(x_rows, at, 3, 0),
                    lax.dynamic_slice_in_dim(bc_rows, at, 3, 0),
                ],
                axis=1,
            )
        )
    lasts = jnp.stack(lasts, axis=0)
    left_at = jnp.sum(jnp.where(homes == left_index, slot_iota, 0))
    right_at = jnp.sum(jnp.where(homes == right_index, slot_iota, 0))
    back_right = shifted(taken(finals, left_at).astype(BF16), "dp", -1)
    back_left = shifted(taken(finals, right_at).astype(BF16), "dp", 1)
    last_right = shifted(taken(lasts, left_at), "dp", -1)
    last_left = shifted(taken(lasts, right_at), "dp", 1)

    def gathered(mine, right, left):
        pieces = []
        for s in range(SLOTS):
            at = jnp.sum(jnp.where(conv_ids == my_index * SLOTS + s, slot_iota, 0))
            there = jnp.where(my_dest[s] == right_index, right, left).astype(F32)
            here = taken(mine, at).astype(F32)
            pieces.append(jnp.where(my_dest[s] == my_index, here, there))
        return jnp.concatenate(pieces, axis=0)

    new_ssm = gathered(finals, back_right, back_left).reshape(ssm_state.shape)
    new_conv = gathered(lasts, last_right, last_left)
    return (y_out, new_ssm, new_conv[:, :, :channels], new_conv[:, :, channels:])


def solution(mesh):
    in_specs = (
        P(("dp", "tensor"), None),
        P(("dp", "tensor"), None),
        P(("dp", "tensor"), None),
        P(("dp", "tensor"), None),
        P(None, "tensor"),
        P(None, "tensor"),
        P("tensor"),
        P("tensor"),
        P("tensor"),
        P("tensor"),
        P("dp", "tensor", None, None),
        P("dp", None, "tensor"),
        P("dp", None, "tensor"),
        P(),
        P(),
        P(),
    )
    out_specs = (
        P("dp", "tensor"),
        P("dp", "tensor", None, None),
        P("dp", None, "tensor"),
        P("dp", None, "tensor"),
    )
    return jax.shard_map(shards, mesh=mesh, in_specs=in_specs, out_specs=out_specs, check_vma=False)
```

```python
import functools

import jax
import jax.numpy as jnp
from jax import lax
from jax.experimental import pallas as pl
from jax.experimental.pallas import tpu as pltpu
from jax.sharding import PartitionSpec as P

HEADS = 128
HEADDIM = 64
STATE = 128
GROUPS = 8
SLOTS = 4
PER_GROUP = HEADS // GROUPS
WIDTH = PER_GROUP * HEADDIM
CHUNK = 256
LANES = 128
EPSILON = 1e-05
LOG2E = 1.4426950408889634
F32 = jnp.float32
BF16 = jnp.bfloat16
best_precision = lax.Precision.HIGHEST


def silu(value):
    half = 0.5 * value
    return half + half * jnp.tanh(half)


def parts_of(value, count):
    parts = []
    for _ in range(count):
        part = value.astype(BF16)
        parts.append(part)
        value = value - part.astype(F32)
    return jnp.concatenate(parts, axis=-1)


def dot(a, b):
    return jnp.dot(a, b, preferred_element_type=F32)


def scan_kernel(
    idx_ref,
    x_ref,
    bc_ref,
    dt_ref,
    log_ref,
    segc_ref,
    segr_ref,
    pos_ref,
    pick_ref,
    fix_x_ref,
    fix_bc_ref,
    par_x_ref,
    par_bc_ref,
    skip_ref,
    spread_ref,
    init0,
    init1,
    init2,
    init3,
    y_ref,
    fin_ref,
    state,
    xs,
    bs,
    xb,
    inter,
):
    chunk = pl.program_id(1)
    inits = (init0, init1, init2, init3)

    @pl.when(chunk == 0)
    def _():
        for k in range(SLOTS):
            state[k * STATE : (k + 1) * STATE, :] = inits[k][0].T
        xs[0:8, :] = jnp.zeros((8, xs.shape[1]), F32)
        bs[0:8, :] = jnp.zeros((8, bs.shape[1]), F32)

    @pl.when(chunk > 0)
    def _():
        xs[0:8, :] = xs[CHUNK : CHUNK + 8, :]
        bs[0:8, :] = bs[CHUNK : CHUNK + 8, :]

    xs[8 : CHUNK + 8, :] = x_ref[...].astype(F32)
    bs[8 : CHUNK + 8, :] = bc_ref[...].astype(F32)
    pos = pos_ref[...]
    pick = pick_ref[...]

    def conv(src, par_ref, fix_ref, lo):
        cols = slice(lo, lo + LANES)
        total = dot(pick, fix_ref[:, cols]) + par_ref[4:5, cols]
        total = total + par_ref[3:4, cols] * src[8 : CHUNK + 8, cols]
        for lag in (1, 2, 3):
            before = jnp.where(pos >= lag, src[8 - lag : CHUNK + 8 - lag, cols], 0.0)
            total = total + par_ref[3 - lag : 4 - lag, cols] * before
        return silu(total)

    for lo in range(0, WIDTH, LANES):
        xb[:, lo : lo + LANES] = conv(xs, par_x_ref, fix_x_ref, lo).astype(BF16)
    b_half = conv(bs, par_bc_ref, fix_bc_ref, 0).astype(BF16)
    c_half = conv(bs, par_bc_ref, fix_bc_ref, STATE).astype(BF16)
    b_wide = b_half.astype(F32)
    c_wide = c_half.astype(F32)

    segc = segc_ref[...]
    segr = segr_ref[0:1, :]
    same = jnp.concatenate([segc, segc], axis=1) == segr
    row = lax.broadcasted_iota(jnp.int32, (CHUNK, CHUNK), 0)
    col = lax.broadcasted_iota(jnp.int32, (CHUNK, CHUNK), 1)
    tri = same & (col <= row)
    upto = jnp.where(tri, 1.0, 0.0).astype(BF16)
    after = jnp.where(same & (col > row), 1.0, 0.0).astype(BF16)
    slot = lax.broadcasted_iota(jnp.int32, (8, CHUNK), 0).astype(F32)
    owned = jnp.where(slot == segr, 1.0, 0.0).astype(BF16)

    logs = parts_of(log_ref[0], 3)

    def summed(mask):
        three = dot(mask, logs)
        return three[:, :LANES] + three[:, LANES : 2 * LANES] + three[:, 2 * LANES :]

    spread = spread_ref[...]

    def expanded(value):
        return dot(parts_of(value, 2), spread)

    dt = dt_ref[0]
    grown = summed(upto)
    back = (grown - jnp.log2(dt)).T
    into = expanded(jnp.exp2(summed(after)) * dt)
    keep = expanded(jnp.exp2(summed(owned)))

    mix = lax.dot_general(c_half, b_half, (((1,), (1,)), ((), ())), preferred_element_type=F32)
    mix = jnp.where(tri, mix, 0.0)
    c_slots = jnp.concatenate(
        [jnp.where(segc == k, c_wide, 0.0).astype(BF16) for k in range(SLOTS)], axis=1
    )
    inter[...] = dot(c_slots, state[...].astype(BF16)) * expanded(jnp.exp2(grown))

    b_turned = b_wide.T
    b_slots = jnp.concatenate(
        [jnp.where(segr == k, b_turned, 0.0).astype(BF16) for k in range(SLOTS)], axis=0
    )
    carried = (xb[...].astype(F32) * into).astype(BF16)
    update = dot(b_slots, carried)
    for k in range(SLOTS):
        rows = slice(k * STATE, (k + 1) * STATE)
        state[rows, :] = state[rows, :] * keep[k : k + 1, :] + update[rows, :]

    left_lanes = lax.broadcasted_iota(jnp.int32, (CHUNK, LANES), 1) < HEADDIM
    for pair in range(PER_GROUP // 2):
        cols = slice(pair * LANES, (pair + 1) * LANES)
        xp = xb[:, cols]
        both = []
        for h in (2 * pair, 2 * pair + 1):
            gap = jnp.minimum(grown[:, h : h + 1] - back[h : h + 1, :], 64.0)
            both.append(dot((mix * jnp.exp2(gap)).astype(BF16), xp))
        y = jnp.where(left_lanes, both[0], both[1])
        y_ref[:, cols] = y + inter[:, cols] + skip_ref[0:1, cols] * xp.astype(F32)

    @pl.when(chunk == pl.num_programs(1) - 1)
    def _():
        for k in range(SLOTS):
            fin_ref[k] = state[k * STATE : (k + 1) * STATE, :].T


def gate_kernel(y_ref, z_ref, gain_ref, out_ref):
    gated = y_ref[...] * silu(z_ref[...].astype(F32))
    square = jnp.mean(gated * gated, axis=1, keepdims=True)
    out_ref[...] = (gated * lax.rsqrt(square + EPSILON) * gain_ref[...]).astype(BF16)


def run_scan(idx, mixed, groups, dt, logs, segc, segr, pos, pick, fix_x, fix_bc, par_x, par_bc, skip, states):
    rows = mixed.shape[0]
    bc_first = groups * WIDTH // (2 * STATE)
    chunks = rows // CHUNK
    heads = jnp.arange(2 * LANES, dtype=jnp.int32)[:, None] % LANES
    spread = (heads == jnp.arange(WIDTH, dtype=jnp.int32)[None, :] // HEADDIM).astype(BF16)

    def by_rows(width):
        return pl.BlockSpec((CHUNK, width), lambda g, c, idx: (c, 0))

    def by_both(width):
        return pl.BlockSpec((CHUNK, width), lambda g, c, idx: (c, g))

    def by_group(height, width):
        return pl.BlockSpec((height, width), lambda g, c, idx: (0, g))

    def init(k):
        return pl.BlockSpec((1, WIDTH, STATE), lambda g, c, idx: (idx[k], g, 0))

    per_group = pl.BlockSpec((1, CHUNK, LANES), lambda g, c, idx: (g, c, 0))
    grid_spec = pltpu.PrefetchScalarGridSpec(
        num_scalar_prefetch=1,
        grid=(groups, chunks),
        in_specs=[
            by_both(WIDTH),
            pl.BlockSpec((CHUNK, 2 * STATE), lambda g, c, idx: (c, bc_first + g)),
            per_group,
            per_group,
            by_rows(LANES),
            pl.BlockSpec((8, CHUNK), lambda g, c, idx: (0, c)),
            by_rows(LANES),
            by_rows(32),
            by_group(32, WIDTH),
            by_group(32, 2 * STATE),
            by_group(5, WIDTH),
            by_group(5, 2 * STATE),
            by_group(1, WIDTH),
            pl.BlockSpec((2 * LANES, WIDTH), lambda g, c, idx: (0, 0)),
            init(0),
            init(1),
            init(2),
            init(3),
        ],
        out_specs=[
            by_both(WIDTH),
            pl.BlockSpec((SLOTS, WIDTH, STATE), lambda g, c, idx: (0, g, 0)),
        ],
        scratch_shapes=[
            pltpu.VMEM((SLOTS * STATE, WIDTH), F32),
            pltpu.VMEM((CHUNK + 8, WIDTH), F32),
            pltpu.VMEM((CHUNK + 8, 2 * STATE), F32),
            pltpu.VMEM((CHUNK, WIDTH), BF16),
            pltpu.VMEM((CHUNK, WIDTH), F32),
        ],
    )
    return pl.pallas_call(
        scan_kernel,
        grid_spec=grid_spec,
        out_shape=[
            jax.ShapeDtypeStruct((rows, groups * WIDTH), F32),
            jax.ShapeDtypeStruct((SLOTS, groups * WIDTH, STATE), F32),
        ],
        compiler_params=pltpu.CompilerParams(
            dimension_semantics=("arbitrary", "arbitrary"), vmem_limit_bytes=48 << 20
        ),
        cost_estimate=pl.CostEstimate(
            flops=40_000_000_000, bytes_accessed=30 << 20, transcendentals=20_000_000
        ),
        name="scan",
    )(idx, mixed, mixed, dt, logs, segc, segr, pos, pick, fix_x, fix_bc, par_x, par_bc, skip, spread, states, states, states, states)


def run_gate(y, z_rows, gain):
    rows, width = y.shape
    block = pl.BlockSpec((CHUNK, WIDTH), lambda g, c: (c, g))
    return pl.pallas_call(
        gate_kernel,
        grid=(width // WIDTH, rows // CHUNK),
        in_specs=[block, block, pl.BlockSpec((1, WIDTH), lambda g, c: (0, g))],
        out_specs=block,
        out_shape=jax.ShapeDtypeStruct((rows, width), BF16),
        compiler_params=pltpu.CompilerParams(
            dimension_semantics=("arbitrary", "arbitrary"), vmem_limit_bytes=56 << 20
        ),
        cost_estimate=pl.CostEstimate(
            flops=40_000_000, bytes_accessed=16 << 20, transcendentals=2_000_000
        ),
        name="gate",
    )(y, z_rows, gain[None, :])


def shifted(value, axis, steps):
    count = lax.axis_size(axis)
    pairs = [(source, (source + steps) % count) for source in range(count)]
    return lax.ppermute(value, axis, pairs)


def exchanged(value):
    got = lax.all_to_all(value, "tensor", split_axis=0, concat_axis=0, tiled=True)
    return got.reshape(-1, value.shape[2])


def plan_rows(owner_idx, lengths, prefill_owner, row_start):
    match = prefill_owner == owner_idx
    earlier = match[None, :] & (row_start[None, :] < row_start[:, None])
    rank = jnp.sum(earlier.astype(jnp.int32), axis=1)
    chosen = match[None, :] & (rank[None, :] == jnp.arange(SLOTS, dtype=jnp.int32)[:, None])

    def pick(values):
        return jnp.sum(jnp.where(chosen, values[None, :], 0), axis=1)

    ids = jnp.arange(prefill_owner.shape[0], dtype=jnp.int32)
    return pick(ids), pick(row_start), pick(lengths)


def fixes(param, state):
    rows = []
    for at in range(3):
        rows.append(sum(param[3 - lag][None, :] * state[:, 3 - lag + at] for lag in range(at + 1, 4)))
    fix = jnp.stack(rows, axis=1).reshape(SLOTS * 3, -1)
    fix = jnp.pad(fix, ((0, 4), (0, 0)))
    high = fix.astype(BF16)
    low = (fix - lax.optimization_barrier(high).astype(F32)).astype(BF16)
    return jnp.concatenate([high, low], axis=0)


def shards(
    x_in,
    z_in,
    bc_in,
    dt_in,
    conv_x_param,
    conv_bc_param,
    decay_rate,
    dt_bias,
    skip_gain,
    norm_gain,
    ssm_state,
    conv_x_state,
    conv_bc_state,
    lengths,
    prefill_owner,
    row_start,
):
    dp_count = lax.axis_size("dp")
    my_index = lax.axis_index("dp")
    left_index = (my_index + dp_count - 1) % dp_count
    right_index = (my_index + 1) % dp_count
    slot_iota = jnp.arange(SLOTS, dtype=jnp.int32)
    my_dest = lax.dynamic_slice_in_dim(prefill_owner, my_index * SLOTS, SLOTS)
    right_slot = jnp.sum(jnp.where(my_dest == right_index, slot_iota, 0))
    left_slot = jnp.sum(jnp.where(my_dest == left_index, slot_iota, 0))
    conv_ids, starts, seg_lengths = plan_rows(my_index, lengths, prefill_owner, row_start)
    homes = conv_ids // SLOTS

    heads = ssm_state.shape[1]
    channels = heads * HEADDIM
    groups = heads // PER_GROUP
    own = ssm_state.reshape(SLOTS, channels, STATE)
    own_conv = jnp.concatenate([conv_x_state, conv_bc_state], axis=2)

    def taken(array, index):
        return lax.dynamic_slice_in_dim(array, index, 1, 0)

    from_left = shifted(taken(own, right_slot), "dp", 1)
    from_right = shifted(taken(own, left_slot), "dp", -1)
    conv_left = shifted(taken(own_conv, right_slot), "dp", 1)
    conv_right = shifted(taken(own_conv, left_slot), "dp", -1)

    tensor_count = lax.axis_size("tensor")
    bc_width = groups * 2 * STATE

    def by_target(value):
        return jnp.transpose(value.reshape(value.shape[0], tensor_count, -1), (1, 0, 2))

    dt_parts = jnp.pad(by_target(dt_in), ((0, 0), (0, 0), (0, -heads % LANES)))
    mixed = exchanged(jnp.concatenate([by_target(x_in), by_target(bc_in), dt_parts], axis=2))
    z_tied, mixed = lax.optimization_barrier((by_target(z_in), mixed))
    z_rows = exchanged(z_tied)
    row_count = mixed.shape[0]
    dt_rows = mixed[:, channels + bc_width : channels + bc_width + heads]

    states = jnp.concatenate([own, from_left, from_right], axis=0)
    where_from = jnp.where(
        homes == my_index, conv_ids % SLOTS, jnp.where(homes == left_index, SLOTS, SLOTS + 1)
    ).astype(jnp.int32)
    convs = jnp.concatenate([own_conv, conv_left, conv_right], axis=0)
    initial_conv = jnp.concatenate([taken(convs, where_from[k]) for k in range(SLOTS)], axis=0)

    row_idx = jnp.arange(row_count, dtype=jnp.int32)
    segment = jnp.sum((row_idx[:, None] >= starts[None, :]).astype(jnp.int32), axis=1) - 1
    begin = jnp.max(jnp.where(row_idx[:, None] >= starts[None, :], starts[None, :], 0), axis=1)
    position = row_idx - begin
    segc = jnp.broadcast_to(segment.astype(F32)[:, None], (row_count, LANES))
    segr = jnp.broadcast_to(segment.astype(F32)[None, :], (8, row_count))
    pos = jnp.broadcast_to(position[:, None], (row_count, LANES))
    code = jnp.where(position < 3, segment * 3 + position, 15)
    pick = (code[:, None] == jnp.arange(32, dtype=jnp.int32)[None, :] % 16).astype(BF16)

    def grouped(value, fill):
        value = jnp.transpose(value.reshape(row_count, groups, PER_GROUP), (1, 0, 2))
        return jnp.pad(value, ((0, 0), (0, 0), (0, LANES - PER_GROUP)), constant_values=fill)

    dt = jax.nn.softplus(dt_rows.astype(F32) + dt_bias[None, :])
    logs = dt * (decay_rate * (-LOG2E))[None, :]
    y, finals = run_scan(
        where_from,
        mixed,
        groups,
        grouped(dt, 1.0),
        grouped(logs, 0.0),
        segc,
        segr,
        pos,
        pick,
        fixes(conv_x_param, initial_conv[:, :, :channels]),
        fixes(conv_bc_param, initial_conv[:, :, channels:]),
        conv_x_param,
        conv_bc_param,
        jnp.repeat(skip_gain, HEADDIM)[None, :],
        states,
    )
    y_out = run_gate(y, z_rows, norm_gain)

    lasts = []
    for k in range(SLOTS):
        at = starts[k] + seg_lengths[k] - 3
        lasts.append(lax.dynamic_slice(mixed, (at, 0), (3, channels + bc_width)))
    lasts = jnp.stack(lasts, axis=0)
    left_at = jnp.sum(jnp.where(homes == left_index, slot_iota, 0))
    right_at = jnp.sum(jnp.where(homes == right_index, slot_iota, 0))
    back_right = shifted(taken(finals, left_at).astype(BF16), "dp", -1)
    back_left = shifted(taken(finals, right_at).astype(BF16), "dp", 1)
    last_right = shifted(taken(lasts, left_at), "dp", -1)
    last_left = shifted(taken(lasts, right_at), "dp", 1)

    def gathered(mine, right, left):
        pieces = []
        for s in range(SLOTS):
            at = jnp.sum(jnp.where(conv_ids == my_index * SLOTS + s, slot_iota, 0))
            there = jnp.where(my_dest[s] == right_index, right, left).astype(F32)
            here = taken(mine, at).astype(F32)
            pieces.append(jnp.where(my_dest[s] == my_index, here, there))
        return jnp.concatenate(pieces, axis=0)

    new_ssm = gathered(finals, back_right, back_left).reshape(ssm_state.shape)
    new_conv = gathered(lasts, last_right, last_left)
    return (y_out, new_ssm, new_conv[:, :, :channels], new_conv[:, :, channels:])


def solution(mesh):
    in_specs = (
        P(("dp", "tensor"), None),
        P(("dp", "tensor"), None),
        P(("dp", "tensor"), None),
        P(("dp", "tensor"), None),
        P(None, "tensor"),
        P(None, "tensor"),
        P("tensor"),
        P("tensor"),
        P("tensor"),
        P("tensor"),
        P("dp", "tensor", None, None),
        P("dp", None, "tensor"),
        P("dp", None, "tensor"),
        P(),
        P(),
        P(),
    )
    out_specs = (
        P("dp", "tensor"),
        P("dp", "tensor", None, None),
        P("dp", None, "tensor"),
        P("dp", None, "tensor"),
    )
    return jax.shard_map(shards, mesh=mesh, in_specs=in_specs, out_specs=out_specs, check_vma=False)
```
